128 devices in a mesh: section: 8 (over x, z_lo), work: 16 (over y, z_hi, core).
Axes of the slice: x: 4, y: 4, z: 4 (z_hi: 2, z_lo: 2; z = z_hi * 2 + z_lo), core: 2. Of those that a mesh axis runs over, the one named last changes fastest.
Arguments:
- queries: bfloat16 [8, 8192, 4096], P('section', 'work')
- new_keys: bfloat16 [8, 8192, 512], P('section', 'work')
- new_values: bfloat16 [8, 8192, 512], P('section', 'work'), may hold values from -6 to 6
- cache_keys: bfloat16 [8, 256, 128, 512], P('section', 'work'), may hold values from -6 to 6
- cache_values: bfloat16 [8, 256, 128, 512], P('section', 'work'), may hold values from -6 to 6
- block_ids: int32 [8, 16, 4], P('section'), may hold values from 0 to 255, as said below
- block_counts: int32 [8, 16], P('section'), may hold values from 3 to 4
Outputs:
- handed: bfloat16 [8, 8192, 4096], P('section', 'work')
The draws below stay inside these ranges and needn't reach their ends.
Inputs may be any that keep to these rules, and one draw needn't show every extreme that they name: `block_ids`: block id b of a section lies on the device of index b // 16 along work; the first block_counts entries of a list are its prefix, the rest are ignored; the ids of one list lie on different devices.
All inputs are finite; a program needn't handle non-finite values.
Results may differ from the reference program's by a relative error of at most 0.006.
Values may be sent and summed in bfloat16 or wider, within the bound.
A program may use at most 192 MiB of HBM per device.

```python
import jax
import jax.numpy as jnp
from jax import lax

H = 32
KVH = 4
HD = 128
C = 512
BT = 128
MAXB = 4
BLK_DEV = 16
SECTIONS = 8
TOKENS = 8192
BLOCKS = 256
N_WORK = 16


def draw_queries(key, part):
    key = jax.random.fold_in(key, 31)
    workers = TOKENS // C
    shape = (SECTIONS, workers, C, KVH, H // KVH, HD)
    values = jnp.clip(2.0 * jax.random.normal(key, shape, jnp.float32), -12.0, 12.0)
    return values.reshape(SECTIONS, TOKENS, H * HD).astype(jnp.bfloat16)


def draw_new_keys(key, part):
    key = jax.random.fold_in(key, 32)
    workers = TOKENS // C
    shape = (SECTIONS, workers, C, KVH, HD)
    values = jnp.clip(jax.random.normal(key, shape, jnp.float32), -6.0, 6.0)
    return values.reshape(SECTIONS, TOKENS, KVH * HD).astype(jnp.bfloat16)


def draw_block_ids(key, part):
    key = jax.random.fold_in(key, 21)
    workers = TOKENS // C
    lists = SECTIONS * workers
    order_keys = jax.random.split(key, lists + 1)

    def spread(subkey):
        return jax.random.permutation(subkey, workers)[:MAXB]
    holders = jax.vmap(spread)(order_keys[1:])
    within = jax.random.randint(order_keys[0], (lists, MAXB), 0, BLK_DEV)
    return (holders * BLK_DEV + within).astype(jnp.int32).reshape(SECTIONS, workers, MAXB)


def draw_block_counts(key, part):
    key = jax.random.fold_in(key, 22)
    workers = TOKENS // C
    lists = SECTIONS * workers
    lowest = max(1, 3 * MAXB // 4)
    primary, second, tertiary = jax.random.split(key, 3)
    counts = jax.random.randint(primary, (lists,), lowest, MAXB + 1)
    longest = jax.random.randint(second, (), 0, lists)
    shortest = (longest + 1 + jax.random.randint(tertiary, (), 0, lists - 1)) % lists
    places = jnp.arange(lists)
    counts = jnp.where(places == longest, MAXB, counts)
    counts = jnp.where(places == shortest, lowest, counts)
    return counts.astype(jnp.int32).reshape(SECTIONS, workers)


def steps_of(rng, dims, pieces, smallest, high):
    def one(position, blocks):
        steps = jax.random.uniform(jax.random.fold_in(jax.random.fold_in(rng, 6), position), (blocks,), jnp.float32, smallest / len(pieces), high / len(pieces))
        return jnp.repeat(jnp.exp(steps), dims[position] // blocks).reshape((-1,) + (1,) * (len(dims) - position - 1))

    level = one(*pieces[0])
    for cut in pieces[1:]:
        level = level * one(*cut)
    return level


def normal_values(own_key, extent, scale, limit, cuts=(), kind=jnp.bfloat16):
    level = steps_of(own_key, extent, cuts, -0.22, 0.18) if cuts else 1.0
    values = jax.random.normal(own_key, extent, jnp.float32) * scale * level
    return jnp.minimum(jnp.maximum(values, -limit), limit).astype(kind)


def setup_inputs(seed: int = 0) -> dict:
    splits = jax.random.split(jax.random.key(seed), 8)
    queries = draw_queries(jax.random.fold_in(splits[7], 71), 0)
    new_keys = draw_new_keys(jax.random.fold_in(splits[7], 71), 0)
    new_values = normal_values(splits[2], (SECTIONS, TOKENS, KVH * HD), 1.0, 6.0, ((0, 8), (1, 16)))
    cache_keys = normal_values(splits[3], (SECTIONS, BLOCKS, BT, KVH * HD), 1.0, 6.0, ((0, 8), (1, 16)))
    cache_values = normal_values(splits[4], (SECTIONS, BLOCKS, BT, KVH * HD), 1.0, 6.0, ((0, 8), (1, 16)))
    block_ids = draw_block_ids(jax.random.fold_in(splits[7], 71), 0)
    block_counts = draw_block_counts(jax.random.fold_in(splits[7], 71), 0)
    return dict(queries=queries, new_keys=new_keys, new_values=new_values, cache_keys=cache_keys, cache_values=cache_values, block_ids=block_ids, block_counts=block_counts)


def span_context(query_rows, fresh_keys, fresh_values, prefix_keys, prefix_values, prefix_count):
    tokens = query_rows.shape[0]
    groups = H // KVH
    keys_all = jnp.concatenate([prefix_keys.reshape(MAXB * BT, KVH * HD), fresh_keys], 0)
    keys_all = keys_all.astype(jnp.float32).reshape(MAXB * BT + tokens, KVH, HD)
    values_all = jnp.concatenate([prefix_values.reshape(MAXB * BT, KVH * HD), fresh_values], 0)
    values_all = values_all.astype(jnp.float32).reshape(MAXB * BT + tokens, KVH, HD)
    grouped = query_rows.astype(jnp.float32).reshape(tokens, KVH, groups, HD)
    scores = jnp.einsum("ckgd,lkd->kgcl", grouped, keys_all) * (HD ** -0.5)
    block_live = jnp.repeat(jnp.arange(MAXB, dtype=jnp.int32) < prefix_count, BT)
    positions = jnp.arange(tokens, dtype=jnp.int32)
    causal = positions[None, :] <= positions[:, None]
    allowed = jnp.concatenate([jnp.broadcast_to(block_live[None, :], (tokens, MAXB * BT)), causal], 1)
    scores = jnp.where(allowed, scores, -1e30)
    row_peak = jnp.max(scores, -1, keepdims=True)
    raw_weights = jnp.exp(scores - row_peak)
    row_total = jnp.sum(raw_weights, -1, keepdims=True)
    weights = lax.optimization_barrier(raw_weights.astype(jnp.bfloat16)).astype(jnp.float32)
    mixed_heads = jnp.einsum("kgcl,lkd->kgcd", weights, values_all) / row_total
    return jnp.transpose(mixed_heads, (2, 0, 1, 3)).reshape(tokens, H * HD).astype(jnp.bfloat16)


def reference(queries, new_keys, new_values, cache_keys, cache_values, block_ids, block_counts):
    spans = SECTIONS * N_WORK
    pool_k = cache_keys.reshape(SECTIONS * BLOCKS, BT, KVH * HD)
    pool_v = cache_values.reshape(SECTIONS * BLOCKS, BT, KVH * HD)
    offsets = (jnp.arange(SECTIONS, dtype=jnp.int32) * BLOCKS)[:, None, None]
    global_ids = (block_ids + offsets).astype(jnp.int32).reshape(spans, MAXB)

    def one_span(inputs):
        query_rows, fresh_keys, fresh_values, listed, prefix_count = inputs
        return span_context(query_rows, fresh_keys, fresh_values, pool_k[listed], pool_v[listed], prefix_count)

    context = lax.map(one_span, (queries.reshape(spans, C, H * HD),
                                  new_keys.reshape(spans, C, KVH * HD),
                                  new_values.reshape(spans, C, KVH * HD),
                                  global_ids,
                                  block_counts.reshape(spans)))
    context = context.reshape(SECTIONS, TOKENS, H * HD)
    return jnp.roll(context, 1, axis=0)
```

```python
import jax
import jax.numpy as jnp
from jax import lax
from jax.experimental import pallas as pl
from jax.experimental.pallas import tpu as pltpu
from jax.sharding import PartitionSpec as P

MESH = pl.DeviceIdType.MESH
HD = 128
BT = 128
MAXB = 4
HELD = 16
C = 512
KVH = 4
GROUP = 8
SECTIONS = 8
Y = 4
NEAR = 2 * Y
TILE = 256
SCALE = HD ** (-0.5) * 1.4426950408889634
EXCLUDED = -1e30


def place():
    work = lax.axis_index("work")
    return lax.axis_index("section"), work // 4, lax.rem(work // 2, 2), lax.rem(work, 2)


def device(section, y, half, core):
    return (lax.rem(section, SECTIONS), (lax.rem(y, Y) * 2 + half) * 2 + core)


def kernel(
    ids, counts, queries, new_keys, new_values, cache_keys, cache_values, out,
    held_keys, held_values, query, keys, values, context, staged, near, pool, picked, far,
    load_sem, query_sem, own_sem, near_sem, pool_sem, far_sem, staged_sem, picked_sem,
    relay_send, relay_recv,
):
    section, y, half, core = place()
    me = (y * 2 + half) * 2 + core
    spot = y * 2 + core
    other_half = 1 - half
    ahead = device(section + 1, y, half, core)
    behind = device(section + SECTIONS - 1, y, half, core)
    across = device(section, y, other_half, core)
    mates = [(y, 1 - core)] + [(lax.rem(y + step, Y), side) for side in (0, 1) for step in (1, 3, 2)]

    loads, query_loads, own_loads = [], [], []
    for g in range(KVH):
        cut = pl.ds(g * HD, HD)
        loads.append([
            pltpu.make_async_copy(cache_keys.at[0, :, :, cut], held_keys[g], load_sem.at[g, 0]),
            pltpu.make_async_copy(cache_values.at[0, :, :, cut], held_values[g], load_sem.at[g, 1]),
        ])
        span = pl.ds(MAXB * BT, C)
        own_loads.append([
            pltpu.make_async_copy(new_keys.at[0, :, cut], keys.at[g, span], own_sem.at[g, 0]),
            pltpu.make_async_copy(new_values.at[0, :, cut], values.at[g, span, pl.ds(0, HD)], own_sem.at[g, 1]),
        ])
        wide = pl.ds(g * GROUP * HD, GROUP * HD)
        query_loads.append(pltpu.make_async_copy(queries.at[0, :, wide], query.at[:, wide], query_sem.at[g]))
    for g in range(KVH):
        for copy in loads[g]:
            copy.start()
    for g in range(KVH):
        for copy in own_loads[g]:
            copy.start()
        query_loads[g].start()

    barrier = pltpu.get_barrier_semaphore()
    greeted = [device(section, my, half, mc) for my, mc in mates] + [ahead, behind, across]
    for other in greeted:
        pl.semaphore_signal(barrier, 1, device_id=other, device_id_type=MESH)

    def listed_here(owner):
        slot = jnp.int32(0)
        for j in range(MAXB):
            offset = ids[0, owner, j] - me * HELD
            hit = (offset >= 0) & (offset < HELD) & (j < counts[0, owner])
            slot = jnp.where(hit, offset, slot)
        return slot

    def holder(owner, j):
        index = lax.shift_right_logical(ids[0, owner, j], 4)
        return (
            lax.shift_right_logical(index, 2) * 2 + (index & 1),
            lax.shift_right_logical(index, 1) & 1,
        )

    slots = [
        (listed_here((my * 2 + other_half) * 2 + mc), listed_here((my * 2 + half) * 2 + mc))
        for my, mc in mates
    ]
    own_slots = (listed_here((y * 2 + other_half) * 2 + core), listed_here(me))

    def sends(g, i):
        my, mc = mates[i]
        to = device(section, my, half, mc)
        return [
            pltpu.make_async_remote_copy(
                src_ref=staged[g].at[i, k],
                dst_ref=(pool, near)[k][g].at[spot],
                send_sem=staged_sem.at[g],
                recv_sem=(pool_sem, near_sem)[k].at[g],
                device_id=to,
                device_id_type=MESH,
            )
            for k in (0, 1)
        ]

    def stage(g):
        for copy in loads[g]:
            copy.wait()
        for i, pair in enumerate(slots):
            for k in (0, 1):
                staged[g][i, k, 0] = held_keys[g][pair[k]]
                staged[g][i, k, 1] = held_values[g][pair[k]]
        for k, buffer in enumerate((pool, near)):
            buffer[g][spot, 0] = held_keys[g][own_slots[k]]
            buffer[g][spot, 1] = held_values[g][own_slots[k]]

    def send_staged(g):
        for i in range(len(mates)):
            for copy in sends(g, i):
                copy.start()

    stage(0)
    pl.semaphore_wait(barrier, len(greeted))
    send_staged(0)
    for g in range(1, KVH):
        stage(g)
        send_staged(g)

    def arrived(buffer, sem, g):
        part = buffer[g].at[pl.ds(0, NEAR - 1)]
        pltpu.make_async_remote_copy(
            src_ref=part, dst_ref=part, send_sem=staged_sem.at[g], recv_sem=sem.at[g],
            device_id=across, device_id_type=MESH,
        ).wait_recv()

    def pass_on(g):
        return pltpu.make_async_remote_copy(
            src_ref=picked[g], dst_ref=far[g], send_sem=picked_sem.at[g], recv_sem=far_sem.at[g],
            device_id=across, device_id_type=MESH,
        )

    def pick(g):
        arrived(pool, pool_sem, g)
        owner = (y * 2 + other_half) * 2 + core
        for j in range(MAXB):
            picked[g][j] = pool[g][holder(owner, j)[0]]
        pass_on(g).start()

    def assemble(g):
        arrived(near, near_sem, g)
        pass_on(g).wait_recv()
        for copy in own_loads[g]:
            copy.wait()
        query_loads[g].wait()
        ones = jnp.ones((BT, HD), jnp.bfloat16)
        first = None
        for j in range(MAXB):
            where, side = holder(me, j)
            block = jnp.where(side == half, near[g][where], far[g][j])
            rows = pl.ds(j * BT, BT)
            if j < MAXB - 1:
                first = block[0] if first is None else first
                keys[g, rows] = block[0]
                values[g, rows, pl.ds(0, HD)] = block[1]
                values[g, rows, pl.ds(HD, HD)] = ones
            else:
                live = j < counts[0, me]
                keys[g, rows] = jnp.where(live, block[0], first)
                values[g, rows, pl.ds(0, HD)] = jnp.where(live, block[1], jnp.zeros_like(block[1]))
                values[g, rows, pl.ds(HD, HD)] = jnp.where(live, ones, jnp.zeros_like(ones))
        values[g, pl.ds(MAXB * BT, C), pl.ds(HD, HD)] = jnp.ones((C, HD), jnp.bfloat16)

    def attend(g, low, high):
        row = lax.broadcasted_iota(jnp.int32, (TILE, TILE), 0)
        column = lax.broadcasted_iota(jnp.int32, (TILE, TILE), 1)
        visible = column <= row

        def head(h, carry):
            cut = pl.ds(pl.multiple_of((g * GROUP + h) * HD, HD), HD)
            for t in range(C // TILE):
                rows = pl.ds(t * TILE, TILE)
                seen = MAXB * BT + (t + 1) * TILE
                scores = lax.dot_general(
                    query[rows, cut], keys[g, pl.ds(0, seen)], (((1,), (1,)), ((), ())),
                    preferred_element_type=jnp.float32,
                )
                last = jnp.where(visible, scores[:, seen - TILE :], EXCLUDED)
                scores = jnp.concatenate([scores[:, : seen - TILE], last], 1)
                peak = jnp.max(scores, 1, keepdims=True)
                weights = jnp.exp2((scores - peak) * SCALE).astype(jnp.bfloat16)
                summed = jnp.dot(weights, values[g, pl.ds(0, seen)], preferred_element_type=jnp.float32)
                context[rows, cut] = (summed[:, :HD] / summed[:, HD:]).astype(jnp.bfloat16)
            pltpu.make_async_remote_copy(
                src_ref=context.at[:, cut], dst_ref=out.at[0, :, cut], send_sem=relay_send, recv_sem=relay_recv,
                device_id=ahead, device_id_type=MESH,
            ).start()
            return carry

        lax.fori_loop(low, high, head, 0)

    pick(0)
    for g in range(KVH):
        assemble(g)
        attend(g, 0, GROUP // 2)
        if g + 1 < KVH:
            pick(g + 1)
        attend(g, GROUP // 2, GROUP)

    for g in range(KVH):
        pltpu.make_async_remote_copy(
            src_ref=staged[g], dst_ref=staged[g], send_sem=staged_sem.at[g], recv_sem=near_sem.at[g],
            device_id=across, device_id_type=MESH,
        ).wait_send()
        pass_on(g).wait_send()
    pltpu.make_async_remote_copy(
        src_ref=context, dst_ref=out.at[0], send_sem=relay_send, recv_sem=relay_recv,
        device_id=ahead, device_id_type=MESH,
    ).wait()


def shards(queries, new_keys, new_values, cache_keys, cache_values, block_ids, block_counts):
    block = (2, BT, HD)
    each = lambda shape: [pltpu.VMEM(shape, jnp.bfloat16)] * KVH
    return pl.pallas_call(
        kernel,
        out_shape=jax.ShapeDtypeStruct(queries.shape, jnp.bfloat16),
        in_specs=[pl.BlockSpec(memory_space=pltpu.SMEM)] * 2 + [pl.BlockSpec(memory_space=pl.ANY)] * 5,
        out_specs=pl.BlockSpec(memory_space=pl.ANY),
        scratch_shapes=[
            each((HELD, BT, HD)),
            each((HELD, BT, HD)),
            pltpu.VMEM((C, KVH * GROUP * HD), jnp.bfloat16),
            pltpu.VMEM((KVH, MAXB * BT + C, HD), jnp.bfloat16),
            pltpu.VMEM((KVH, MAXB * BT + C, 2 * HD), jnp.bfloat16),
            pltpu.VMEM((C, KVH * GROUP * HD), jnp.bfloat16),
            each((NEAR - 1, 2) + block),
            each((NEAR,) + block),
            each((NEAR,) + block),
            each((MAXB,) + block),
            each((MAXB,) + block),
            pltpu.SemaphoreType.DMA((KVH, 2)),
            pltpu.SemaphoreType.DMA((KVH,)),
            pltpu.SemaphoreType.DMA((KVH, 2)),
            pltpu.SemaphoreType.DMA((KVH,)),
            pltpu.SemaphoreType.DMA((KVH,)),
            pltpu.SemaphoreType.DMA((KVH,)),
            pltpu.SemaphoreType.DMA((KVH,)),
            pltpu.SemaphoreType.DMA((KVH,)),
            pltpu.SemaphoreType.DMA,
            pltpu.SemaphoreType.DMA,
        ],
        compiler_params=pltpu.CompilerParams(
            collective_id=0, has_side_effects=True, vmem_limit_bytes=60 * 2**20
        ),
        cost_estimate=pl.CostEstimate(
            flops=4 * 32 * C * (MAXB * BT + C) * HD,
            bytes_accessed=24 * 2**20,
            transcendentals=32 * C * (MAXB * BT + C),
        ),
        name="relayed_attention",
    )(block_ids, block_counts, queries, new_keys, new_values, cache_keys, cache_values)


def solution(mesh):
    in_specs = (
        P("section", "work", None),
        P("section", "work", None),
        P("section", "work", None),
        P("section", "work", None, None),
        P("section", "work", None, None),
        P("section", None, None),
        P("section", None),
    )
    out_specs = P("section", "work", None)
    return jax.shard_map(shards, mesh=mesh, in_specs=in_specs, out_specs=out_specs, check_vma=False)
```

```python
import jax
import jax.numpy as jnp
from jax import lax
from jax.experimental import pallas as pl
from jax.experimental.pallas import tpu as pltpu
from jax.sharding import PartitionSpec as P

MESH = pl.DeviceIdType.MESH
HD = 128
BT = 128
MAXB = 4
HELD = 16
C = 512
KVH = 4
GROUP = 8
SECTIONS = 8
Y = 4
NEAR = 2 * Y
TILE = 256
SCALE = HD ** (-0.5) * 1.4426950408889634
EXCLUDED = -1e30


def place():
    work = lax.axis_index("work")
    return lax.axis_index("section"), work // 4, lax.rem(work // 2, 2), lax.rem(work, 2)


def device(section, y, half, core):
    return (lax.rem(section, SECTIONS), (lax.rem(y, Y) * 2 + half) * 2 + core)


def kernel(
    ids, counts, queries, new_keys, new_values, cache_keys, cache_values, out,
    held_keys, held_values, query, keys, values, context, staged, near, pool, picked, far,
    load_sem, query_sem, own_sem, near_sem, pool_sem, far_sem, staged_sem, picked_sem,
    relay_send, relay_recv,
):
    section, y, half, core = place()
    me = (y * 2 + half) * 2 + core
    spot = y * 2 + core
    other_half = 1 - half
    ahead = device(section + 1, y, half, core)
    behind = device(section + SECTIONS - 1, y, half, core)
    across = device(section, y, other_half, core)
    mates = [(y, 1 - core)] + [(lax.rem(y + step, Y), side) for side in (0, 1) for step in (1, 3, 2)]

    loads, query_loads, own_loads = [], [], []
    for g in range(KVH):
        cut = pl.ds(g * HD, HD)
        loads.append([
            pltpu.make_async_copy(cache_keys.at[0, :, :, cut], held_keys[g], load_sem.at[g, 0]),
            pltpu.make_async_copy(cache_values.at[0, :, :, cut], held_values[g], load_sem.at[g, 1]),
        ])
        span = pl.ds(MAXB * BT, C)
        own_loads.append([
            pltpu.make_async_copy(new_keys.at[0, :, cut], keys.at[g, span], own_sem.at[g, 0]),
            pltpu.make_async_copy(new_values.at[0, :, cut], values.at[g, span, pl.ds(0, HD)], own_sem.at[g, 1]),
        ])
        wide = pl.ds(g * GROUP * HD, GROUP * HD)
        query_loads.append(pltpu.make_async_copy(queries.at[0, :, wide], query.at[:, wide], query_sem.at[g]))
    for g in range(KVH):
        for copy in loads[g]:
            copy.start()
    for g in range(KVH):
        for copy in own_loads[g]:
            copy.start()
        query_loads[g].start()

    barrier = pltpu.get_barrier_semaphore()
    greeted = [device(section, my, half, mc) for my, mc in mates] + [ahead, behind, across]
    for other in greeted:
        pl.semaphore_signal(barrier, 1, device_id=other, device_id_type=MESH)

    def listed_here(owner):
        slot = jnp.int32(0)
        for j in range(MAXB):
            offset = ids[0, j, owner] - me * HELD
            hit = (offset >= 0) & (offset < HELD) & (j < counts[0, owner])
            slot = jnp.where(hit, offset, slot)
        return slot

    def holder(owner, j):
        index = lax.shift_right_logical(ids[0, j, owner], 4)
        return (
            lax.shift_right_logical(index, 2) * 2 + (index & 1),
            lax.shift_right_logical(index, 1) & 1,
        )

    slots = [
        (listed_here((my * 2 + other_half) * 2 + mc), listed_here((my * 2 + half) * 2 + mc))
        for my, mc in mates
    ]
    own_slots = (listed_here((y * 2 + other_half) * 2 + core), listed_here(me))

    def stage(g, k):
        for i, pair in enumerate(slots):
            staged[g][i, k, 0] = held_keys[g][pair[k]]
            staged[g][i, k, 1] = held_values[g][pair[k]]
        buffer = (pool, near)[k][g]
        buffer[spot, 0] = held_keys[g][own_slots[k]]
        buffer[spot, 1] = held_values[g][own_slots[k]]

    def send_staged(g, k):
        for i, (my, mc) in enumerate(mates):
            pltpu.make_async_remote_copy(
                src_ref=staged[g].at[i, k],
                dst_ref=(pool, near)[k][g].at[spot],
                send_sem=staged_sem.at[g],
                recv_sem=(pool_sem, near_sem)[k].at[g],
                device_id=device(section, my, half, mc),
                device_id_type=MESH,
            ).start()

    for g in range(KVH):
        for copy in loads[g]:
            copy.wait()
        stage(g, 0)
        if g == 0:
            pl.semaphore_wait(barrier, len(greeted))
        send_staged(g, 0)
    for g in range(KVH):
        stage(g, 1)
        send_staged(g, 1)

    def arrived(buffer, sem, g):
        part = buffer[g].at[pl.ds(0, NEAR - 1)]
        pltpu.make_async_remote_copy(
            src_ref=part, dst_ref=part, send_sem=staged_sem.at[g], recv_sem=sem.at[g],
            device_id=across, device_id_type=MESH,
        ).wait_recv()

    def pass_on(g):
        return pltpu.make_async_remote_copy(
            src_ref=picked[g], dst_ref=far[g], send_sem=picked_sem.at[g], recv_sem=far_sem.at[g],
            device_id=across, device_id_type=MESH,
        )

    def pick(g):
        arrived(pool, pool_sem, g)
        owner = (y * 2 + other_half) * 2 + core
        for j in range(MAXB):
            picked[g][j] = pool[g][holder(owner, j)[0]]
        pass_on(g).start()

    def assemble(g):
        arrived(near, near_sem, g)
        pass_on(g).wait_recv()
        for copy in own_loads[g]:
            copy.wait()
        query_loads[g].wait()
        ones = jnp.ones((BT, HD), jnp.bfloat16)
        first = None
        for j in range(MAXB):
            where, side = holder(me, j)
            block = jnp.where(side == half, near[g][where], far[g][j])
            rows = pl.ds(j * BT, BT)
            if j < MAXB - 1:
                first = block[0] if first is None else first
                keys[g, rows] = block[0]
                values[g, rows, pl.ds(0, HD)] = block[1]
                values[g, rows, pl.ds(HD, HD)] = ones
            else:
                live = j < counts[0, me]
                keys[g, rows] = jnp.where(live, block[0], first)
                values[g, rows, pl.ds(0, HD)] = jnp.where(live, block[1], jnp.zeros_like(block[1]))
                values[g, rows, pl.ds(HD, HD)] = jnp.where(live, ones, jnp.zeros_like(ones))
        values[g, pl.ds(MAXB * BT, C), pl.ds(HD, HD)] = jnp.ones((C, HD), jnp.bfloat16)

    def attend(g):
        row = lax.broadcasted_iota(jnp.int32, (TILE, TILE), 0)
        column = lax.broadcasted_iota(jnp.int32, (TILE, TILE), 1)
        visible = column <= row

        def head(h, carry):
            cut = pl.ds(pl.multiple_of((g * GROUP + h) * HD, HD), HD)
            for t in range(C // TILE):
                rows = pl.ds(t * TILE, TILE)
                seen = MAXB * BT + (t + 1) * TILE
                scores = lax.dot_general(
                    query[rows, cut], keys[g, pl.ds(0, seen)], (((1,), (1,)), ((), ())),
                    preferred_element_type=jnp.float32,
                )
                last = jnp.where(visible, scores[:, seen - TILE :], EXCLUDED)
                scores = jnp.concatenate([scores[:, : seen - TILE], last], 1)
                peak = jnp.max(scores, 1, keepdims=True)
                weights = jnp.exp2((scores - peak) * SCALE).astype(jnp.bfloat16)
                summed = jnp.dot(weights, values[g, pl.ds(0, seen)], preferred_element_type=jnp.float32)
                context[rows, cut] = (summed[:, :HD] / summed[:, HD:]).astype(jnp.bfloat16)
            pltpu.make_async_remote_copy(
                src_ref=context.at[:, cut], dst_ref=out.at[0, :, cut], send_sem=relay_send, recv_sem=relay_recv,
                device_id=ahead, device_id_type=MESH,
            ).start()
            return carry

        lax.fori_loop(0, GROUP, head, 0)

    for g in range(KVH):
        pick(g)
    for g in range(KVH):
        assemble(g)
        attend(g)

    for g in range(KVH):
        pltpu.make_async_remote_copy(
            src_ref=staged[g], dst_ref=staged[g], send_sem=staged_sem.at[g], recv_sem=near_sem.at[g],
            device_id=across, device_id_type=MESH,
        ).wait_send()
        pass_on(g).wait_send()
    pltpu.make_async_remote_copy(
        src_ref=context, dst_ref=out.at[0], send_sem=relay_send, recv_sem=relay_recv,
        device_id=ahead, device_id_type=MESH,
    ).wait()


def shards(queries, new_keys, new_values, cache_keys, cache_values, block_ids, block_counts):
    block = (2, BT, HD)
    each = lambda shape: [pltpu.VMEM(shape, jnp.bfloat16)] * KVH
    return pl.pallas_call(
        kernel,
        out_shape=pltpu.VMEM(queries.shape, jnp.bfloat16),
        in_specs=[pl.BlockSpec(memory_space=pltpu.SMEM)] * 2 + [pl.BlockSpec(memory_space=pl.ANY)] * 5,
        out_specs=pl.BlockSpec(memory_space=pltpu.VMEM),
        scratch_shapes=[
            each((HELD, BT, HD)),
            each((HELD, BT, HD)),
            pltpu.VMEM((C, KVH * GROUP * HD), jnp.bfloat16),
            pltpu.VMEM((KVH, MAXB * BT + C, HD), jnp.bfloat16),
            pltpu.VMEM((KVH, MAXB * BT + C, 2 * HD), jnp.bfloat16),
            pltpu.VMEM((C, KVH * GROUP * HD), jnp.bfloat16),
            each((NEAR - 1, 2) + block),
            each((NEAR,) + block),
            each((NEAR,) + block),
            each((MAXB,) + block),
            each((MAXB,) + block),
            pltpu.SemaphoreType.DMA((KVH, 2)),
            pltpu.SemaphoreType.DMA((KVH,)),
            pltpu.SemaphoreType.DMA((KVH, 2)),
            pltpu.SemaphoreType.DMA((KVH,)),
            pltpu.SemaphoreType.DMA((KVH,)),
            pltpu.SemaphoreType.DMA((KVH,)),
            pltpu.SemaphoreType.DMA((KVH,)),
            pltpu.SemaphoreType.DMA((KVH,)),
            pltpu.SemaphoreType.DMA,
            pltpu.SemaphoreType.DMA,
        ],
        compiler_params=pltpu.CompilerParams(
            collective_id=0, has_side_effects=True, vmem_limit_bytes=59 * 2**20
        ),
        cost_estimate=pl.CostEstimate(
            flops=4 * 32 * C * (MAXB * BT + C) * HD,
            bytes_accessed=24 * 2**20,
            transcendentals=32 * C * (MAXB * BT + C),
        ),
        name="relayed_attention",
    )(jnp.swapaxes(block_ids, 1, 2), block_counts, queries, new_keys, new_values, cache_keys, cache_values)


def solution(mesh):
    in_specs = (
        P("section", "work", None),
        P("section", "work", None),
        P("section", "work", None),
        P("section", "work", None, None),
        P("section", "work", None, None),
        P("section", None, None),
        P("section", None),
    )
    out_specs = P("section", "work", None)
    return jax.shard_map(shards, mesh=mesh, in_specs=in_specs, out_specs=out_specs, check_vma=False)
```

```python
import jax
import jax.numpy as jnp
from jax import lax
from jax.experimental import pallas as pl
from jax.experimental.pallas import tpu as pltpu
from jax.sharding import PartitionSpec as P

MESH = pl.DeviceIdType.MESH
HD = 128
BT = 128
MAXB = 4
HELD = 16
C = 512
KVH = 4
GROUP = 8
SECTIONS = 8
Y = 4
NEAR = 2 * Y
TILE = 256
SCALE = HD ** (-0.5) * 1.4426950408889634
EXCLUDED = -1e30


def place():
    work = lax.axis_index("work")
    return lax.axis_index("section"), work // 4, lax.rem(work // 2, 2), lax.rem(work, 2)


def device(section, y, half, core):
    return (lax.rem(section, SECTIONS), (lax.rem(y, Y) * 2 + half) * 2 + core)


def kernel(
    ids, counts, queries, new_keys, new_values, cache_keys, cache_values, out,
    held_keys, held_values, query, keys, values, context, near_out, far_out, near, pool, picked, far,
    load_sem, query_sem, own_sem, near_sem, pool_sem, far_sem, near_sent, far_sent, picked_sent,
    relay_send, relay_recv,
):
    section, y, half, core = place()
    me = (y * 2 + half) * 2 + core
    spot = y * 2 + core
    other_half = 1 - half
    ahead = device(section + 1, y, half, core)
    behind = device(section + SECTIONS - 1, y, half, core)
    served = lax.rem(y + 1 + 2 * core, Y)
    server = lax.rem(y + 3 - 2 * core, Y)
    onward = device(section, served, other_half, core)
    mates = [(y, 1 - core)] + [(lax.rem(y + step, Y), side) for side in (0, 1) for step in (1, 3, 2)]
    others = [(lax.rem(y + step, Y), side) for side in (0, 1) for step in (0, 1, 3, 2)]

    loads, query_loads, own_loads = [], [], []
    for g in range(KVH):
        cut = pl.ds(g * HD, HD)
        loads.append([
            pltpu.make_async_copy(cache_keys.at[0, :, :, cut], held_keys[g], load_sem.at[g, 0]),
            pltpu.make_async_copy(cache_values.at[0, :, :, cut], held_values[g], load_sem.at[g, 1]),
        ])
        span = pl.ds(MAXB * BT, C)
        own_loads.append([
            pltpu.make_async_copy(new_keys.at[0, :, cut], keys.at[g, span], own_sem.at[g, 0]),
            pltpu.make_async_copy(new_values.at[0, :, cut], values.at[g, span, pl.ds(0, HD)], own_sem.at[g, 1]),
        ])
        wide = pl.ds(g * GROUP * HD, GROUP * HD)
        query_loads.append(pltpu.make_async_copy(queries.at[0, :, wide], query.at[:, wide], query_sem.at[g]))
    for g in range(KVH):
        for copy in loads[g]:
            copy.start()
    for g in range(KVH):
        for copy in own_loads[g]:
            copy.start()
        query_loads[g].start()

    barrier = pltpu.get_barrier_semaphore()
    greeted = [device(section, my, half, mc) for my, mc in mates] + [ahead, behind]
    greeted += [device(section, my, other_half, mc) for my, mc in others]
    for other in greeted:
        pl.semaphore_signal(barrier, 1, device_id=other, device_id_type=MESH)

    def listed_here(owner):
        slot = jnp.int32(0)
        for j in range(MAXB):
            offset = ids[0, j, owner] - me * HELD
            hit = (offset >= 0) & (offset < HELD) & (j < counts[0, owner])
            slot = jnp.where(hit, offset, slot)
        return slot

    def holder(owner, j):
        index = lax.shift_right_logical(ids[0, j, owner], 4)
        return (
            lax.shift_right_logical(index, 2) * 2 + (index & 1),
            lax.shift_right_logical(index, 1) & 1,
        )

    def put(target, g, slot):
        target[0] = held_keys[g][slot]
        target[1] = held_values[g][slot]

    def send(source, target, sent, arrived, to):
        pltpu.make_async_remote_copy(
            src_ref=source, dst_ref=target, send_sem=sent, recv_sem=arrived, device_id=to, device_id_type=MESH
        ).start()

    near_slots = [listed_here((my * 2 + half) * 2 + mc) for my, mc in mates]

    def stage_near(g):
        for i, slot in enumerate(near_slots):
            put(near_out[g].at[i], g, slot)
        put(near[g].at[spot], g, listed_here(me))

    def send_near(g, chosen):
        for i in chosen:
            my, mc = mates[i]
            send(near_out[g].at[i], near[g].at[spot], near_sent.at[g], near_sem.at[g], device(section, my, half, mc))

    def stage_pool(g):
        for i, slot in enumerate(pool_slots):
            put(far_out[g].at[i], g, slot)
        put(pool[g].at[spot], g, listed_here((served * 2 + other_half) * 2 + core))

    def send_pool(g):
        for i, (my, mc) in enumerate(mates):
            send(far_out[g].at[i], pool[g].at[spot], far_sent.at[g], pool_sem.at[g], device(section, my, half, mc))

    for copy in loads[0]:
        copy.wait()
    stage_near(0)
    for i, (my, mc) in enumerate(others):
        put(far_out[0].at[i], 0, listed_here((my * 2 + other_half) * 2 + mc))
    pl.semaphore_wait(barrier, len(greeted))
    send_near(0, [0])
    for side in (0, 1):
        send_near(0, range(1 + 3 * side, 4 + 3 * side))
        for i in range(4 * side, 4 * side + 4):
            my, mc = others[i]
            send(
                far_out[0].at[i], far[0].at[spot], far_sent.at[0], far_sem.at[0],
                device(section, my, other_half, mc),
            )

    pool_slots = [
        listed_here((lax.rem(my + 1 + 2 * mc, Y) * 2 + other_half) * 2 + mc) for my, mc in mates
    ]

    def exchange(g):
        for copy in loads[g]:
            copy.wait()
        stage_pool(g)
        send_pool(g)
        stage_near(g)
        send_near(g, range(len(mates)))

    exchange(1)

    def arrived(part, sem):
        pltpu.make_async_remote_copy(
            src_ref=part, dst_ref=part, send_sem=far_sent.at[0], recv_sem=sem, device_id=ahead, device_id_type=MESH
        ).wait_recv()

    def left(part, sem):
        pltpu.make_async_remote_copy(
            src_ref=part, dst_ref=part, send_sem=sem, recv_sem=far_sem.at[0], device_id=ahead, device_id_type=MESH
        ).wait_send()

    def pick(g):
        arrived(pool[g].at[pl.ds(0, NEAR - 1)], pool_sem.at[g])
        owner = (served * 2 + other_half) * 2 + core
        for j in range(MAXB):
            picked[g][j] = pool[g][holder(owner, j)[0]]
        send(picked[g], far[g], picked_sent.at[g], far_sem.at[g], onward)

    def assemble(g):
        arrived(near[g].at[pl.ds(0, NEAR - 1)], near_sem.at[g])
        arrived(far[g], far_sem.at[g])
        for copy in own_loads[g]:
            copy.wait()
        query_loads[g].wait()
        ones = jnp.ones((BT, HD), jnp.bfloat16)
        first = None
        for j in range(MAXB):
            where, side = holder(me, j)
            block = jnp.where(side == half, near[g][where], far[g][where if g == 0 else j])
            rows = pl.ds(j * BT, BT)
            if j < MAXB - 1:
                first = block[0] if first is None else first
                keys[g, rows] = block[0]
                values[g, rows, pl.ds(0, HD)] = block[1]
                values[g, rows, pl.ds(HD, HD)] = ones
            else:
                live = j < counts[0, me]
                keys[g, rows] = jnp.where(live, block[0], first)
                values[g, rows, pl.ds(0, HD)] = jnp.where(live, block[1], jnp.zeros_like(block[1]))
                values[g, rows, pl.ds(HD, HD)] = jnp.where(live, ones, jnp.zeros_like(ones))
        values[g, pl.ds(MAXB * BT, C), pl.ds(HD, HD)] = jnp.ones((C, HD), jnp.bfloat16)

    def attend(g):
        row = lax.broadcasted_iota(jnp.int32, (TILE, TILE), 0)
        column = lax.broadcasted_iota(jnp.int32, (TILE, TILE), 1)
        visible = column <= row

        def head(h, carry):
            cut = pl.ds(pl.multiple_of((g * GROUP + h) * HD, HD), HD)
            for t in range(C // TILE):
                rows = pl.ds(t * TILE, TILE)
                seen = MAXB * BT + (t + 1) * TILE
                scores = lax.dot_general(
                    query[rows, cut], keys[g, pl.ds(0, seen)], (((1,), (1,)), ((), ())),
                    preferred_element_type=jnp.float32,
                )
                last = jnp.where(visible, scores[:, seen - TILE :], EXCLUDED)
                scores = jnp.concatenate([scores[:, : seen - TILE], last], 1)
                peak = jnp.max(scores, 1, keepdims=True)
                weights = jnp.exp2((scores - peak) * SCALE).astype(jnp.bfloat16)
                summed = jnp.dot(weights, values[g, pl.ds(0, seen)], preferred_element_type=jnp.float32)
                context[rows, cut] = (summed[:, :HD] / summed[:, HD:]).astype(jnp.bfloat16)
            pltpu.make_async_remote_copy(
                src_ref=context.at[:, cut], dst_ref=out.at[0, :, cut], send_sem=relay_send, recv_sem=relay_recv,
                device_id=ahead, device_id_type=MESH,
            ).start()
            return carry

        lax.fori_loop(0, GROUP, head, 0)

    for g in range(KVH):
        assemble(g)
        attend(g)
        if g + 1 < KVH:
            pick(g + 1)
        if g + 2 < KVH:
            exchange(g + 2)

    for g in range(KVH):
        left(near_out[g], near_sent.at[g])
        left(far_out[g], far_sent.at[g])
        if g > 0:
            left(picked[g], picked_sent.at[g])
    pltpu.make_async_remote_copy(
        src_ref=context, dst_ref=out.at[0], send_sem=relay_send, recv_sem=relay_recv,
        device_id=ahead, device_id_type=MESH,
    ).wait()


def shards(queries, new_keys, new_values, cache_keys, cache_values, block_ids, block_counts):
    block = (2, BT, HD)
    each = lambda shape: [pltpu.VMEM(shape, jnp.bfloat16)] * KVH
    first_and = lambda one, rest: [pltpu.VMEM(one, jnp.bfloat16)] + [pltpu.VMEM(rest, jnp.bfloat16)] * (KVH - 1)
    return pl.pallas_call(
        kernel,
        out_shape=pltpu.VMEM(queries.shape, jnp.bfloat16),
        in_specs=[pl.BlockSpec(memory_space=pltpu.SMEM)] * 2 + [pl.BlockSpec(memory_space=pl.ANY)] * 5,
        out_specs=pl.BlockSpec(memory_space=pltpu.VMEM),
        scratch_shapes=[
            each((HELD, BT, HD)),
            each((HELD, BT, HD)),
            pltpu.VMEM((C, KVH * GROUP * HD), jnp.bfloat16),
            pltpu.VMEM((KVH, MAXB * BT + C, HD), jnp.bfloat16),
            pltpu.VMEM((KVH, MAXB * BT + C, 2 * HD), jnp.bfloat16),
            pltpu.VMEM((C, KVH * GROUP * HD), jnp.bfloat16),
            each((NEAR - 1,) + block),
            first_and((NEAR,) + block, (NEAR - 1,) + block),
            each((NEAR,) + block),
            first_and((1,) + block, (NEAR,) + block),
            first_and((1,) + block, (MAXB,) + block),
            first_and((NEAR,) + block, (MAXB,) + block),
            pltpu.SemaphoreType.DMA((KVH, 2)),
            pltpu.SemaphoreType.DMA((KVH,)),
            pltpu.SemaphoreType.DMA((KVH, 2)),
            pltpu.SemaphoreType.DMA((KVH,)),
            pltpu.SemaphoreType.DMA((KVH,)),
            pltpu.SemaphoreType.DMA((KVH,)),
            pltpu.SemaphoreType.DMA((KVH,)),
            pltpu.SemaphoreType.DMA((KVH,)),
            pltpu.SemaphoreType.DMA((KVH,)),
            pltpu.SemaphoreType.DMA,
            pltpu.SemaphoreType.DMA,
        ],
        compiler_params=pltpu.CompilerParams(
            collective_id=0, has_side_effects=True, vmem_limit_bytes=59 * 2**20
        ),
        cost_estimate=pl.CostEstimate(
            flops=4 * 32 * C * (MAXB * BT + C) * HD,
            bytes_accessed=24 * 2**20,
            transcendentals=32 * C * (MAXB * BT + C),
        ),
        name="relayed_attention",
    )(jnp.swapaxes(block_ids, 1, 2), block_counts, queries, new_keys, new_values, cache_keys, cache_values)


def solution(mesh):
    in_specs = (
        P("section", "work", None),
        P("section", "work", None),
        P("section", "work", None),
        P("section", "work", None, None),
        P("section", "work", None, None),
        P("section", None, None),
        P("section", None),
    )
    out_specs = P("section", "work", None)
    return jax.shard_map(shards, mesh=mesh, in_specs=in_specs, out_specs=out_specs, check_vma=False)
```

```python
import jax
import jax.numpy as jnp
from jax import lax
from jax.experimental import pallas as pl
from jax.experimental.pallas import tpu as pltpu
from jax.sharding import PartitionSpec as P

MESH = pl.DeviceIdType.MESH
HD = 128
BT = 128
MAXB = 4
HELD = 16
C = 512
KVH = 4
GROUP = 8
SECTIONS = 8
Y = 4
NEAR = 2 * Y
TILE = 256
SCALE = HD ** (-0.5) * 1.4426950408889634
EXCLUDED = -1e30


def place():
    work = lax.axis_index("work")
    return lax.axis_index("section"), work // 4, lax.rem(work // 2, 2), lax.rem(work, 2)


def device(section, y, half, core):
    return (lax.rem(section, SECTIONS), (lax.rem(y, Y) * 2 + half) * 2 + core)


def kernel(
    all_ids, all_counts, queries, new_keys, new_values, cache_keys, cache_values, out,
    ids, counts, held_keys, held_values, query, keys, values, context, near_out, far_out, near, pool, picked, far,
    list_sem, load_sem, query_sem, own_sem, near_sem, pool_sem, far_sem, near_sent, far_sent, picked_sent,
    relay_send, relay_recv,
):
    section, y, half, core = place()
    me = (y * 2 + half) * 2 + core
    spot = y * 2 + core
    other_half = 1 - half
    ahead = device(section + 1, y, half, core)
    behind = device(section + SECTIONS - 1, y, half, core)
    served = lax.rem(y + 1 + 2 * core, Y)
    server = lax.rem(y + 3 - 2 * core, Y)
    onward = device(section, served, other_half, core)
    mates = [(y, 1 - core)] + [(lax.rem(y + step, Y), side) for side in (0, 1) for step in (1, 3, 2)]
    others = [(lax.rem(y + step, Y), side) for side in (0, 1) for step in (0, 1, 3, 2)]

    loads, query_loads, own_loads = [], [], []
    for g in range(KVH):
        cut = pl.ds(g * HD, HD)
        loads.append([
            pltpu.make_async_copy(cache_keys.at[0, :, :, cut], held_keys[g], load_sem.at[g, 0]),
            pltpu.make_async_copy(cache_values.at[0, :, :, cut], held_values[g], load_sem.at[g, 1]),
        ])
        span = pl.ds(MAXB * BT, C)
        own_loads.append([
            pltpu.make_async_copy(new_keys.at[0, :, cut], keys.at[g, span], own_sem.at[g, 0]),
            pltpu.make_async_copy(new_values.at[0, :, cut], values.at[g, span, pl.ds(0, HD)], own_sem.at[g, 1]),
        ])
        wide = pl.ds(g * GROUP * HD, GROUP * HD)
        query_loads.append(pltpu.make_async_copy(queries.at[0, :, wide], query.at[:, wide], query_sem.at[g]))
    lists = [
        pltpu.make_async_copy(all_ids, ids, list_sem.at[0]),
        pltpu.make_async_copy(all_counts, counts, list_sem.at[1]),
    ]
    for copy in lists + loads[0]:
        copy.start()

    barrier = pltpu.get_barrier_semaphore()
    greeted = [device(section, my, half, mc) for my, mc in mates] + [ahead, behind]
    greeted += [device(section, my, other_half, mc) for my, mc in others]
    for other in greeted:
        pl.semaphore_signal(barrier, 1, device_id=other, device_id_type=MESH)

    for copy in lists:
        copy.wait()

    def listed_here(owner):
        slot = jnp.int32(0)
        for j in range(MAXB):
            offset = ids[0, j, owner] - me * HELD
            hit = (offset >= 0) & (offset < HELD) & (j < counts[0, owner])
            slot = jnp.where(hit, offset, slot)
        return slot

    def holder(owner, j):
        index = lax.shift_right_logical(ids[0, j, owner], 4)
        return (
            lax.shift_right_logical(index, 2) * 2 + (index & 1),
            lax.shift_right_logical(index, 1) & 1,
        )

    def put(target, g, slot):
        target[0] = held_keys[g][slot]
        target[1] = held_values[g][slot]

    def send(source, target, sent, arrived, to):
        pltpu.make_async_remote_copy(
            src_ref=source, dst_ref=target, send_sem=sent, recv_sem=arrived, device_id=to, device_id_type=MESH
        ).start()

    near_slots = [listed_here((my * 2 + half) * 2 + mc) for my, mc in mates]

    def stage_near(g):
        for i, slot in enumerate(near_slots):
            put(near_out[g].at[i], g, slot)
        put(near[g].at[spot], g, own_slot)

    def send_near(g, chosen):
        for i in chosen:
            my, mc = mates[i]
            send(near_out[g].at[i], near[g].at[spot], near_sent.at[g], near_sem.at[g], device(section, my, half, mc))

    def stage_pool(g):
        for i, slot in enumerate(pool_slots):
            put(far_out[g].at[i], g, slot)
        put(pool[g].at[spot], g, listed_here((served * 2 + other_half) * 2 + core))

    def send_pool(g):
        for i, (my, mc) in enumerate(mates):
            send(far_out[g].at[i], pool[g].at[spot], far_sent.at[g], pool_sem.at[g], device(section, my, half, mc))

    far_slots = [listed_here((my * 2 + other_half) * 2 + mc) for my, mc in others]
    own_slot = listed_here(me)
    for copy in loads[0]:
        copy.wait()
    for copy in loads[1] + own_loads[0] + [query_loads[0]]:
        copy.start()
    for i, slot in enumerate(far_slots):
        put(far_out[0].at[i], 0, slot)
    stage_near(0)
    pl.semaphore_wait(barrier, len(greeted))
    def send_far(chosen):
        for i in chosen:
            my, mc = others[i]
            send(
                far_out[0].at[i], far[0].at[spot], far_sent.at[0], far_sem.at[0],
                device(section, my, other_half, mc),
            )

    send_near(0, [0])
    send_far((3, 1, 2, 0))
    send_near(0, (3, 1, 2, 4, 5, 6))
    send_far((4, 5, 6, 7))
    for g in range(1, KVH):
        for copy in (loads[g + 1] if g + 1 < KVH else []) + own_loads[g] + [query_loads[g]]:
            copy.start()
    pool_slots = [
        listed_here((lax.rem(my + 1 + 2 * mc, Y) * 2 + other_half) * 2 + mc) for my, mc in mates
    ]

    def exchange(g):
        for copy in loads[g]:
            copy.wait()
        stage_pool(g)
        send_pool(g)
        stage_near(g)
        send_near(g, range(len(mates)))

    def arrived(part, sem):
        pltpu.make_async_remote_copy(
            src_ref=part, dst_ref=part, send_sem=far_sent.at[0], recv_sem=sem, device_id=ahead, device_id_type=MESH
        ).wait_recv()

    def left(part, sem):
        pltpu.make_async_remote_copy(
            src_ref=part, dst_ref=part, send_sem=sem, recv_sem=far_sem.at[0], device_id=ahead, device_id_type=MESH
        ).wait_send()

    def pick(g):
        arrived(pool[g].at[pl.ds(0, NEAR - 1)], pool_sem.at[g])
        owner = (served * 2 + other_half) * 2 + core
        for j in range(MAXB):
            picked[g][j] = pool[g][holder(owner, j)[0]]
        send(picked[g], far[g], picked_sent.at[g], far_sem.at[g], onward)

    def assemble(g):
        arrived(near[g].at[pl.ds(0, NEAR - 1)], near_sem.at[g])
        arrived(far[g], far_sem.at[g])
        for copy in own_loads[g]:
            copy.wait()
        query_loads[g].wait()
        ones = jnp.ones((BT, HD), jnp.bfloat16)
        first = None
        for j in range(MAXB):
            where, side = holder(me, j)
            block = jnp.where(side == half, near[g][where], far[g][where if g == 0 else j])
            rows = pl.ds(j * BT, BT)
            if j < MAXB - 1:
                first = block[0] if first is None else first
                keys[g, rows] = block[0]
                values[g, rows, pl.ds(0, HD)] = block[1]
                values[g, rows, pl.ds(HD, HD)] = ones
            else:
                live = j < counts[0, me]
                keys[g, rows] = jnp.where(live, block[0], first)
                values[g, rows, pl.ds(0, HD)] = jnp.where(live, block[1], jnp.zeros_like(block[1]))
                values[g, rows, pl.ds(HD, HD)] = jnp.where(live, ones, jnp.zeros_like(ones))
        values[g, pl.ds(MAXB * BT, C), pl.ds(HD, HD)] = jnp.ones((C, HD), jnp.bfloat16)

    def attend(g):
        row = lax.broadcasted_iota(jnp.int32, (TILE, TILE), 0)
        column = lax.broadcasted_iota(jnp.int32, (TILE, TILE), 1)
        visible = column <= row

        def head(h, carry):
            cut = pl.ds(pl.multiple_of((g * GROUP + h) * HD, HD), HD)
            for t in range(C // TILE):
                rows = pl.ds(t * TILE, TILE)
                seen = MAXB * BT + (t + 1) * TILE
                scores = lax.dot_general(
                    query[rows, cut], keys[g, pl.ds(0, seen)], (((1,), (1,)), ((), ())),
                    preferred_element_type=jnp.float32,
                )
                last = jnp.where(visible, scores[:, seen - TILE :], EXCLUDED)
                scores = jnp.concatenate([scores[:, : seen - TILE], last], 1)
                peak = jnp.max(scores, 1, keepdims=True)
                weights = jnp.exp2((scores - peak) * SCALE).astype(jnp.bfloat16)
                summed = jnp.dot(weights, values[g, pl.ds(0, seen)], preferred_element_type=jnp.float32)
                context[rows, cut] = (summed[:, :HD] / summed[:, HD:]).astype(jnp.bfloat16)
                send(context.at[rows, cut], out.at[0, rows, cut], relay_send, relay_recv, ahead)
            return carry

        lax.fori_loop(0, GROUP, head, 0)

    for g in range(KVH):
        assemble(g)
        if g == 0:
            exchange(1)
        attend(g)
        if g + 1 < KVH:
            pick(g + 1)
        if g + 2 < KVH:
            exchange(g + 2)

    for g in range(KVH):
        left(near_out[g], near_sent.at[g])
        left(far_out[g], far_sent.at[g])
        if g > 0:
            left(picked[g], picked_sent.at[g])
    pltpu.make_async_remote_copy(
        src_ref=context, dst_ref=out.at[0], send_sem=relay_send, recv_sem=relay_recv,
        device_id=ahead, device_id_type=MESH,
    ).wait()


def shards(queries, new_keys, new_values, cache_keys, cache_values, block_ids, block_counts):
    block = (2, BT, HD)
    each = lambda shape: [pltpu.VMEM(shape, jnp.bfloat16)] * KVH
    first_and = lambda one, rest: [pltpu.VMEM(one, jnp.bfloat16)] + [pltpu.VMEM(rest, jnp.bfloat16)] * (KVH - 1)
    return pl.pallas_call(
        kernel,
        out_shape=pltpu.VMEM(queries.shape, jnp.bfloat16),
        in_specs=[pl.BlockSpec(memory_space=pl.ANY)] * 7,
        out_specs=pl.BlockSpec(memory_space=pltpu.VMEM),
        scratch_shapes=[
            pltpu.SMEM((1,) + (MAXB, block_ids.shape[1]), jnp.int32),
            pltpu.SMEM(block_counts.shape, jnp.int32),
            each((HELD, BT, HD)),
            each((HELD, BT, HD)),
            pltpu.VMEM((C, KVH * GROUP * HD), jnp.bfloat16),
            pltpu.VMEM((KVH, MAXB * BT + C, HD), jnp.bfloat16),
            pltpu.VMEM((KVH, MAXB * BT + C, 2 * HD), jnp.bfloat16),
            pltpu.VMEM((C, KVH * GROUP * HD), jnp.bfloat16),
            each((NEAR - 1,) + block),
            first_and((NEAR,) + block, (NEAR - 1,) + block),
            each((NEAR,) + block),
            first_and((1,) + block, (NEAR,) + block),
            first_and((1,) + block, (MAXB,) + block),
            first_and((NEAR,) + block, (MAXB,) + block),
            pltpu.SemaphoreType.DMA((2,)),
            pltpu.SemaphoreType.DMA((KVH, 2)),
            pltpu.SemaphoreType.DMA((KVH,)),
            pltpu.SemaphoreType.DMA((KVH, 2)),
            pltpu.SemaphoreType.DMA((KVH,)),
            pltpu.SemaphoreType.DMA((KVH,)),
            pltpu.SemaphoreType.DMA((KVH,)),
            pltpu.SemaphoreType.DMA((KVH,)),
            pltpu.SemaphoreType.DMA((KVH,)),
            pltpu.SemaphoreType.DMA((KVH,)),
            pltpu.SemaphoreType.DMA,
            pltpu.SemaphoreType.DMA,
        ],
        compiler_params=pltpu.CompilerParams(
            collective_id=0, has_side_effects=True, vmem_limit_bytes=59 * 2**20
        ),
        cost_estimate=pl.CostEstimate(
            flops=4 * 32 * C * (MAXB * BT + C) * HD,
            bytes_accessed=24 * 2**20,
            transcendentals=32 * C * (MAXB * BT + C),
        ),
        name="relayed_attention",
    )(jnp.swapaxes(block_ids, 1, 2), block_counts, queries, new_keys, new_values, cache_keys, cache_values)


def solution(mesh):
    in_specs = (
        P("section", "work", None),
        P("section", "work", None),
        P("section", "work", None),
        P("section", "work", None, None),
        P("section", "work", None, None),
        P("section", None, None),
        P("section", None),
    )
    out_specs = P("section", "work", None)
    return jax.shard_map(shards, mesh=mesh, in_specs=in_specs, out_specs=out_specs, check_vma=False)
```

```python
import jax
import jax.numpy as jnp
from jax import lax
from jax.experimental import pallas as pl
from jax.experimental.pallas import tpu as pltpu
from jax.sharding import PartitionSpec as P

MESH = pl.DeviceIdType.MESH
HD = 128
BT = 128
MAXB = 4
HELD = 16
C = 512
KVH = 4
GROUP = 8
SECTIONS = 8
Y = 4
NEAR = 2 * Y
TILE = 256
SCALE = HD ** (-0.5) * 1.4426950408889634
EXCLUDED = -1e30


def place():
    work = lax.axis_index("work")
    return lax.axis_index("section"), work // 4, lax.rem(work // 2, 2), lax.rem(work, 2)


def device(section, y, half, core):
    return (lax.rem(section, SECTIONS), (lax.rem(y, Y) * 2 + half) * 2 + core)


def kernel(
    all_ids, all_counts, queries, new_keys, new_values, cache_keys, cache_values, out,
    ids, counts, held_keys, held_values, query, keys, values, context, near_out, far_out, near, pool, picked, far,
    list_sem, load_sem, query_sem, own_sem, near_sem, pool_sem, far_sem, near_sent, far_sent, picked_sent,
    relay_send, relay_recv,
):
    section, y, half, core = place()
    me = (y * 2 + half) * 2 + core
    spot = y * 2 + core
    other_half = 1 - half
    ahead = device(section + 1, y, half, core)
    behind = device(section + SECTIONS - 1, y, half, core)
    served = lax.rem(y + 1 + 2 * core, Y)
    server = lax.rem(y + 3 - 2 * core, Y)
    onward = device(section, served, other_half, core)
    mates = [(y, 1 - core)] + [(lax.rem(y + step, Y), side) for side in (0, 1) for step in (1, 3, 2)]
    others = [(lax.rem(y + step, Y), side) for side in (0, 1) for step in (0, 1, 3, 2)]

    loads, query_loads, own_loads = [], [], []
    for g in range(KVH):
        cut = pl.ds(g * HD, HD)
        loads.append([
            pltpu.make_async_copy(cache_keys.at[0, :, :, cut], held_keys[g], load_sem.at[g, 0]),
            pltpu.make_async_copy(cache_values.at[0, :, :, cut], held_values[g], load_sem.at[g, 1]),
        ])
        span = pl.ds(MAXB * BT, C)
        own_loads.append([
            pltpu.make_async_copy(new_keys.at[0, :, cut], keys.at[g, span], own_sem.at[g, 0]),
            pltpu.make_async_copy(new_values.at[0, :, cut], values.at[g, span, pl.ds(0, HD)], own_sem.at[g, 1]),
        ])
        wide = pl.ds(g * GROUP * HD, GROUP * HD)
        query_loads.append(pltpu.make_async_copy(queries.at[0, :, wide], query.at[:, wide], query_sem.at[g]))
    lists = [
        pltpu.make_async_copy(all_ids, ids, list_sem.at[0]),
        pltpu.make_async_copy(all_counts, counts, list_sem.at[1]),
    ]
    for copy in lists + loads[0]:
        copy.start()

    barrier = pltpu.get_barrier_semaphore()
    greeted = [device(section, my, half, mc) for my, mc in mates] + [ahead, behind]
    greeted += [device(section, my, other_half, mc) for my, mc in others]
    for other in greeted:
        pl.semaphore_signal(barrier, 1, device_id=other, device_id_type=MESH)

    for copy in lists:
        copy.wait()

    def listed_here(owner):
        slot = jnp.int32(0)
        for j in range(MAXB):
            offset = ids[0, j, owner] - me * HELD
            hit = (offset >= 0) & (offset < HELD) & (j < counts[0, owner])
            slot = jnp.where(hit, offset, slot)
        return slot

    def holder(owner, j):
        index = lax.shift_right_logical(ids[0, j, owner], 4)
        return (
            lax.shift_right_logical(index, 2) * 2 + (index & 1),
            lax.shift_right_logical(index, 1) & 1,
        )

    def put(target, g, slot):
        target[0] = held_keys[g][slot]
        target[1] = held_values[g][slot]

    def send(source, target, sent, arrived, to):
        pltpu.make_async_remote_copy(
            src_ref=source, dst_ref=target, send_sem=sent, recv_sem=arrived, device_id=to, device_id_type=MESH
        ).start()

    near_slots = [listed_here((my * 2 + half) * 2 + mc) for my, mc in mates]

    def stage_near(g):
        for i, slot in enumerate(near_slots):
            put(near_out[g].at[i], g, slot)
        put(near[g].at[spot], g, own_slot)

    def send_near(g, chosen):
        for i in chosen:
            my, mc = mates[i]
            send(near_out[g].at[i], near[g].at[spot], near_sent.at[g], near_sem.at[g], device(section, my, half, mc))

    def stage_pool(g):
        for i, slot in enumerate(pool_slots):
            put(far_out[g].at[i], g, slot)
        put(pool[g].at[spot], g, listed_here((served * 2 + other_half) * 2 + core))

    def send_pool(g):
        for i, (my, mc) in enumerate(mates):
            send(far_out[g].at[i], pool[g].at[spot], far_sent.at[g], pool_sem.at[g], device(section, my, half, mc))

    far_slots = [listed_here((my * 2 + other_half) * 2 + mc) for my, mc in others]
    own_slot = listed_here(me)
    for copy in loads[0]:
        copy.wait()
    for copy in loads[1] + own_loads[0] + [query_loads[0]]:
        copy.start()
    for i, slot in enumerate(far_slots):
        put(far_out[0].at[i], 0, slot)
    stage_near(0)
    pl.semaphore_wait(barrier, len(greeted))
    def send_far(chosen):
        for i in chosen:
            my, mc = others[i]
            send(
                far_out[0].at[i], far[0].at[spot], far_sent.at[0], far_sem.at[0],
                device(section, my, other_half, mc),
            )

    send_far((0, 4, 3, 1, 2))
    send_near(0, (0, 3, 1, 2, 4, 5, 6))
    send_far((5, 6, 7))
    for g in range(1, KVH):
        for copy in (loads[g + 1] if g + 1 < KVH else []) + own_loads[g] + [query_loads[g]]:
            copy.start()
    pool_slots = [
        listed_here((lax.rem(my + 1 + 2 * mc, Y) * 2 + other_half) * 2 + mc) for my, mc in mates
    ]

    def exchange(g):
        for copy in loads[g]:
            copy.wait()
        stage_pool(g)
        send_pool(g)
        stage_near(g)
        send_near(g, range(len(mates)))

    def arrived(part, sem):
        pltpu.make_async_remote_copy(
            src_ref=part, dst_ref=part, send_sem=far_sent.at[0], recv_sem=sem, device_id=ahead, device_id_type=MESH
        ).wait_recv()

    def left(part, sem):
        pltpu.make_async_remote_copy(
            src_ref=part, dst_ref=part, send_sem=sem, recv_sem=far_sem.at[0], device_id=ahead, device_id_type=MESH
        ).wait_send()

    def pick(g):
        arrived(pool[g].at[pl.ds(0, NEAR - 1)], pool_sem.at[g])
        owner = (served * 2 + other_half) * 2 + core
        for j in range(MAXB):
            picked[g][j] = pool[g][holder(owner, j)[0]]
        send(picked[g], far[g], picked_sent.at[g], far_sem.at[g], onward)

    def assemble(g):
        arrived(near[g].at[pl.ds(0, NEAR - 1)], near_sem.at[g])
        arrived(far[g], far_sem.at[g])
        for copy in own_loads[g]:
            copy.wait()
        query_loads[g].wait()
        ones = jnp.ones((BT, HD), jnp.bfloat16)
        first = None
        for j in range(MAXB):
            where, side = holder(me, j)
            block = jnp.where(side == half, near[g][where], far[g][where if g == 0 else j])
            rows = pl.ds(j * BT, BT)
            if j < MAXB - 1:
                first = block[0] if first is None else first
                keys[g, rows] = block[0]
                values[g, rows, pl.ds(0, HD)] = block[1]
                values[g, rows, pl.ds(HD, HD)] = ones
            else:
                live = j < counts[0, me]
                keys[g, rows] = jnp.where(live, block[0], first)
                values[g, rows, pl.ds(0, HD)] = jnp.where(live, block[1], jnp.zeros_like(block[1]))
                values[g, rows, pl.ds(HD, HD)] = jnp.where(live, ones, jnp.zeros_like(ones))
        values[g, pl.ds(MAXB * BT, C), pl.ds(HD, HD)] = jnp.ones((C, HD), jnp.bfloat16)

    def attend(g):
        row = lax.broadcasted_iota(jnp.int32, (TILE, TILE), 0)
        column = lax.broadcasted_iota(jnp.int32, (TILE, TILE), 1)
        visible = column <= row

        def head(h, carry):
            cut = pl.ds(pl.multiple_of((g * GROUP + h) * HD, HD), HD)
            for t in range(C // TILE):
                rows = pl.ds(t * TILE, TILE)
                seen = MAXB * BT + (t + 1) * TILE
                scores = lax.dot_general(
                    query[rows, cut], keys[g, pl.ds(0, seen)], (((1,), (1,)), ((), ())),
                    preferred_element_type=jnp.float32,
                )
                last = jnp.where(visible, scores[:, seen - TILE :], EXCLUDED)
                scores = jnp.concatenate([scores[:, : seen - TILE], last], 1)
                peak = jnp.max(scores, 1, keepdims=True)
                weights = jnp.exp2((scores - peak) * SCALE).astype(jnp.bfloat16)
                summed = jnp.dot(weights, values[g, pl.ds(0, seen)], preferred_element_type=jnp.float32)
                context[rows, cut] = (summed[:, :HD] / summed[:, HD:]).astype(jnp.bfloat16)
                send(context.at[rows, cut], out.at[0, rows, cut], relay_send, relay_recv, ahead)
            return carry

        lax.fori_loop(0, GROUP, head, 0)

    for g in range(KVH):
        assemble(g)
        if g == 0:
            exchange(1)
        attend(g)
        if g + 1 < KVH:
            pick(g + 1)
        if g + 2 < KVH:
            exchange(g + 2)

    for g in range(KVH):
        left(near_out[g], near_sent.at[g])
        left(far_out[g], far_sent.at[g])
        if g > 0:
            left(picked[g], picked_sent.at[g])
    pltpu.make_async_remote_copy(
        src_ref=context, dst_ref=out.at[0], send_sem=relay_send, recv_sem=relay_recv,
        device_id=ahead, device_id_type=MESH,
    ).wait()


def shards(queries, new_keys, new_values, cache_keys, cache_values, block_ids, block_counts):
    block = (2, BT, HD)
    each = lambda shape: [pltpu.VMEM(shape, jnp.bfloat16)] * KVH
    first_and = lambda one, rest: [pltpu.VMEM(one, jnp.bfloat16)] + [pltpu.VMEM(rest, jnp.bfloat16)] * (KVH - 1)
    return pl.pallas_call(
        kernel,
        out_shape=pltpu.VMEM(queries.shape, jnp.bfloat16),
        in_specs=[pl.BlockSpec(memory_space=pl.ANY)] * 7,
        out_specs=pl.BlockSpec(memory_space=pltpu.VMEM),
        scratch_shapes=[
            pltpu.SMEM((1,) + (MAXB, block_ids.shape[1]), jnp.int32),
            pltpu.SMEM(block_counts.shape, jnp.int32),
            each((HELD, BT, HD)),
            each((HELD, BT, HD)),
            pltpu.VMEM((C, KVH * GROUP * HD), jnp.bfloat16),
            pltpu.VMEM((KVH, MAXB * BT + C, HD), jnp.bfloat16),
            pltpu.VMEM((KVH, MAXB * BT + C, 2 * HD), jnp.bfloat16),
            pltpu.VMEM((C, KVH * GROUP * HD), jnp.bfloat16),
            each((NEAR - 1,) + block),
            first_and((NEAR,) + block, (NEAR - 1,) + block),
            each((NEAR,) + block),
            first_and((1,) + block, (NEAR,) + block),
            first_and((1,) + block, (MAXB,) + block),
            first_and((NEAR,) + block, (MAXB,) + block),
            pltpu.SemaphoreType.DMA((2,)),
            pltpu.SemaphoreType.DMA((KVH, 2)),
            pltpu.SemaphoreType.DMA((KVH,)),
            pltpu.SemaphoreType.DMA((KVH, 2)),
            pltpu.SemaphoreType.DMA((KVH,)),
            pltpu.SemaphoreType.DMA((KVH,)),
            pltpu.SemaphoreType.DMA((KVH,)),
            pltpu.SemaphoreType.DMA((KVH,)),
            pltpu.SemaphoreType.DMA((KVH,)),
            pltpu.SemaphoreType.DMA((KVH,)),
            pltpu.SemaphoreType.DMA,
            pltpu.SemaphoreType.DMA,
        ],
        compiler_params=pltpu.CompilerParams(
            collective_id=0, has_side_effects=True, vmem_limit_bytes=59 * 2**20
        ),
        cost_estimate=pl.CostEstimate(
            flops=4 * 32 * C * (MAXB * BT + C) * HD,
            bytes_accessed=24 * 2**20,
            transcendentals=32 * C * (MAXB * BT + C),
        ),
        name="relayed_attention",
    )(jnp.swapaxes(block_ids, 1, 2), block_counts, queries, new_keys, new_values, cache_keys, cache_values)


def solution(mesh):
    in_specs = (
        P("section", "work", None),
        P("section", "work", None),
        P("section", "work", None),
        P("section", "work", None, None),
        P("section", "work", None, None),
        P("section", None, None),
        P("section", None),
    )
    out_specs = P("section", "work", None)
    return jax.shard_map(shards, mesh=mesh, in_specs=in_specs, out_specs=out_specs, check_vma=False)
```
